512 devices in a mesh: gx: 32 (over y, x), gy: 16 (over z, core).
Axes of the slice: x: 4, y: 8, z: 8, core: 2. Of those that a mesh axis runs over, the one named last changes fastest.
Arguments:
- tracer_now: float32 [2, 32, 256, 4096], P(None, None, 'gy', 'gx'), may hold values from -6 to 6
- velocity_now: float32 [2, 32, 256, 4096], P(None, None, 'gy', 'gx'), may hold values from -6 to 6
- tracer_old: float32 [2, 32, 256, 4096], P(None, None, 'gy', 'gx'), may hold values from -6 to 6
- velocity_old: float32 [2, 32, 256, 4096], P(None, None, 'gy', 'gx'), may hold values from -6 to 6
- depth_levels: int32 [256, 4096], P('gy', 'gx'), may hold values from 0 to 32
- land_blocks: int32 [32, 512], P('gy', 'gx'), may hold values 0 or 1
Outputs:
- tracer_next: float32 [2, 32, 256, 4096], P(None, None, 'gy', 'gx')
- velocity_next: float32 [2, 32, 256, 4096], P(None, None, 'gy', 'gx')
- surface_height: float32 [256, 4096], P('gy', 'gx')
- residual: float32 [256, 4096], P('gy', 'gx')
The draws below stay inside these ranges and needn't reach their ends.
Inputs may be any that keep to these rules, and one draw needn't show every extreme that they name: `depth_levels`: 0 marks a land column.
All inputs are finite; a program needn't handle non-finite values. No bound on the sum of `land_blocks` on one device may be relied on, other than what follows from the above.
Results may differ from the reference program's by a relative error of at most 0.0003.
Values sent between devices are 32-bit elements; how exact they have to be, the bound alone decides.
No kernel may reach another device: no remote copies, remote signals or barrier semaphores. Data moves between devices by JAX's collectives and lax.ppermute only.
A program may use at most 64 MiB of HBM per device.

```python
import jax
import jax.numpy as jnp
from jax import lax

LEVELS = 32
BLOCK = 8
ITERS = 4
NLAT = 256
NLON = 4096
BLOCKS_LAT = 32
BLOCKS_LON = 512


def plant(values, key, least, high):
    longest = values.shape.index(max(values.shape))
    spots = []
    for shift in (0, 1):
        where = [jax.random.randint(jax.random.fold_in(key, axis), (), 0, length) for axis, length in enumerate(values.shape)]
        where[longest] = (where[longest] + shift) % values.shape[longest]
        spots.append(tuple(where))
    return values.at[spots[0]].set(least).at[spots[1]].set(high)


def shard_levels(own_key, dims, cuts, low, largest):
    level = 1.0
    for position, shards_of in cuts:
        heights = jax.random.uniform(jax.random.fold_in(jax.random.fold_in(own_key, 6), position), (shards_of,), jnp.float32, low / len(cuts), largest / len(cuts))
        level = level * jnp.repeat(jnp.exp(heights), dims[position] // shards_of).reshape((-1,) + (1,) * (len(dims) - 1 - position))
    return level


def normal_values(rng, shape, scale, limit, shards=(), kind=jnp.bfloat16):
    entries = jax.random.normal(rng, shape, jnp.float32) * scale
    if len(shards) > 0:
        entries = shard_levels(rng, shape, shards, -0.22, 0.18) * entries
    return jnp.clip(entries, min=-limit, max=limit).astype(kind)


def setup_inputs(seed: int = 0) -> dict:
    keys = jax.random.split(jax.random.key(seed), 7)
    return {
        "tracer_now": normal_values(keys[0], (2, LEVELS, NLAT, NLON), 1.0, 6.0, ((2, 16), (3, 32)), jnp.float32),
        "velocity_now": normal_values(keys[1], (2, LEVELS, NLAT, NLON), 1.0, 6.0, ((2, 16), (3, 32)), jnp.float32),
        "tracer_old": normal_values(keys[2], (2, LEVELS, NLAT, NLON), 1.0, 6.0, ((2, 16), (3, 32)), jnp.float32),
        "velocity_old": normal_values(keys[3], (2, LEVELS, NLAT, NLON), 1.0, 6.0, ((2, 16), (3, 32)), jnp.float32),
        "depth_levels": plant(jax.random.randint(keys[4], (NLAT, NLON), 0, LEVELS + 1), jax.random.fold_in(keys[4], 1), 0, LEVELS).astype(jnp.int32),
        "land_blocks": plant((jax.random.randint(keys[5], (BLOCKS_LAT, BLOCKS_LON), 0, 4) < 3).astype(jnp.int32), jax.random.fold_in(keys[5], 1), 0, 1),
    }


STEP_TWICE = 0.1
TRACER_MIX = 0.05
MOMENTUM_MIX = 0.05
HEAT_EXPANSION = 0.2
SALT_CONTRACTION = 0.15
PRESSURE_SCALE = 0.2
SURFACE_TERM = 1.0
SIDES = ((0, 1), (0, -1), (1, 0), (-1, 0))
ALL_SIDES = ((0, 1, 1.0), (0, -1, 1.0), (1, 0, 1.0), (-1, 0, 1.0), (1, 1, 0.5), (1, -1, 0.5), (-1, 1, 0.5), (-1, -1, 0.5))


def offset(array, row_step, col_step):
    rows = array.shape[-2] - 2
    cols = array.shape[-1] - 2
    return array[..., 1 + row_step:1 + row_step + rows, 1 + col_step:1 + col_step + cols]


def interior(array):
    return offset(array, 0, 0)


def laplace(field, mask):
    center = interior(field)
    mask_mid = interior(mask)
    result = jnp.zeros_like(center)
    for row_step, col_step in SIDES:
        result = result + mask_mid * offset(mask, row_step, col_step) * (offset(field, row_step, col_step) - center)
    return result


def biharmonic(field, mask):
    first = interior(mask) * laplace(field, mask)
    return laplace(first, interior(mask))


def advect(tracer, eastward, northward, mask):
    center = interior(tracer)
    mask_mid = interior(mask)
    result = jnp.zeros_like(center)
    for row_step, col_step in SIDES:
        speed = northward if row_step != 0 else eastward
        orient = float(row_step + col_step)
        face = mask_mid * offset(mask, row_step, col_step) * 0.5 * (interior(speed) + offset(speed, row_step, col_step))
        result = result + orient * face * 0.5 * (center + offset(tracer, row_step, col_step))
    return result


def gradient(pressure, mask, row_step, col_step):
    center = interior(pressure)
    mask_mid = interior(mask)
    ahead = mask_mid * offset(mask, row_step, col_step) * (offset(pressure, row_step, col_step) - center)
    behind = mask_mid * offset(mask, -row_step, -col_step) * (center - offset(pressure, -row_step, -col_step))
    return 0.5 * (ahead + behind)


def pressure_field(fields):
    density = (-HEAT_EXPANSION * fields[0] + SALT_CONTRACTION * fields[1]) * fields[8]
    return PRESSURE_SCALE * jnp.cumsum(density, axis=0)


def coriolis_rows(first_row, count, rows_global):
    rows = (first_row + jnp.arange(count, dtype=jnp.int32)).astype(jnp.float32)
    return (2.0 * (rows + 0.5) / rows_global - 1.0)[:, None]


def evolve(fields, pressure, coriolis):
    mask_two = fields[8]
    mask_one = interior(mask_two)
    mask_zero = interior(mask_one)
    temp_now = interior(fields[0])
    salt_now = interior(fields[1])
    east_now = interior(fields[2])
    north_now = interior(fields[3])
    press_one = interior(pressure)
    cor_zero = coriolis[2:-2]
    temp_next = mask_zero * (interior(interior(fields[4])) + STEP_TWICE * (-advect(temp_now, east_now, north_now, mask_one) - TRACER_MIX * biharmonic(fields[4], mask_two)))
    salt_next = mask_zero * (interior(interior(fields[5])) + STEP_TWICE * (-advect(salt_now, east_now, north_now, mask_one) - TRACER_MIX * biharmonic(fields[5], mask_two)))
    east_next = mask_zero * (interior(interior(fields[6])) + STEP_TWICE * (cor_zero * interior(north_now) - gradient(press_one, mask_one, 0, 1) - MOMENTUM_MIX * biharmonic(fields[6], mask_two)))
    north_next = mask_zero * (interior(interior(fields[7])) + STEP_TWICE * (-cor_zero * interior(east_now) - gradient(press_one, mask_one, 1, 0) - MOMENTUM_MIX * biharmonic(fields[7], mask_two)))
    return jnp.stack([temp_next, salt_next, east_next, north_next], 0)


def divergence_source(transports, top_band):
    east_part = 0.5 * (offset(transports[0], 0, 1) - offset(transports[0], 0, -1))
    north_part = 0.5 * (offset(transports[1], 1, 0) - offset(transports[1], -1, 0))
    return -interior(top_band) * (east_part + north_part)


def couplings(depth_band, top_band):
    weights = []
    diagonal = jnp.full(interior(depth_band).shape, SURFACE_TERM, jnp.float32)
    for row_step, col_step, factor in ALL_SIDES:
        weight = factor * 0.5 * (interior(depth_band) + offset(depth_band, row_step, col_step)) * interior(top_band) * offset(top_band, row_step, col_step)
        weights.append(weight)
        diagonal = diagonal + weight
    return weights, diagonal


def apply_operator(padded, weights, diagonal):
    result = diagonal * interior(padded)
    for number, (row_step, col_step, factor) in enumerate(ALL_SIDES):
        result = result - weights[number] * offset(padded, row_step, col_step)
    return result


def pad_global(array, width):
    lead = [(0, 0)] * (array.ndim - 1)
    array = jnp.pad(array, lead + [(width, width)], mode="wrap")
    lead = [(0, 0)] * (array.ndim - 2)
    return jnp.pad(array, lead + [(width, width), (0, 0)])


def reference(tracer_now, velocity_now, tracer_old, velocity_old, depth_levels, land_blocks):
    open_cells = jnp.repeat(jnp.repeat(land_blocks, BLOCK, 0), BLOCK, 1).astype(jnp.float32)
    level_index = jnp.arange(LEVELS, dtype=jnp.int32)[:, None, None]
    wet_cells = (level_index < depth_levels[None]).astype(jnp.float32) * open_cells[None]
    fields = jnp.concatenate([tracer_now, velocity_now, tracer_old, velocity_old, wet_cells[None]], 0)
    padded = pad_global(fields, 2)
    pressure = pressure_field(padded)
    coriolis = coriolis_rows(jnp.int32(-2), NLAT + 4, NLAT)

    def one_level(pair):
        return evolve(pair[0], pair[1], coriolis)

    updated = lax.map(one_level, (jnp.moveaxis(padded, 1, 0), pressure))
    updated = jnp.moveaxis(updated, 0, 1)
    transports = pad_global(jnp.sum(updated[2:4], 1) / LEVELS, 1)
    band = pad_global(wet_cells, 1)
    depth_band = jnp.sum(band, 0) / LEVELS
    top_band = band[0]
    source = divergence_source(transports, top_band)
    weights, diagonal = couplings(depth_band, top_band)
    residual = source
    solution = jnp.zeros_like(source)
    direction = jnp.zeros_like(source)
    image_dir = jnp.zeros_like(source)
    descent_old = jnp.float32(1.0)
    step_old = jnp.float32(1.0)
    for iteration in range(ITERS):
        search = residual / diagonal
        image = apply_operator(pad_global(search, 1), weights, diagonal)
        descent = jnp.sum(residual * search)
        curvature = jnp.sum(image * search)
        if iteration == 0:
            blend = jnp.float32(0.0)
            step_length = descent / curvature
        else:
            blend = descent / descent_old
            step_length = descent / (curvature - blend * descent / step_old)
        direction = search + blend * direction
        image_dir = image + blend * image_dir
        solution = solution + step_length * direction
        residual = residual - step_length * image_dir
        descent_old = descent
        step_old = step_length
    return updated[0:2], updated[2:4], solution, residual
```

```python
import jax
import jax.numpy as jnp
from jax import lax
from jax.sharding import PartitionSpec as P

BLOCK = 8
ITERS = 4


STEP_TWICE = 0.1
TRACER_MIX = 0.05
MOMENTUM_MIX = 0.05
HEAT_EXPANSION = 0.2
SALT_CONTRACTION = 0.15
PRESSURE_SCALE = 0.2
SURFACE_TERM = 1.0
SIDES = ((0, 1), (0, -1), (1, 0), (-1, 0))
ALL_SIDES = (
    (0, 1, 1.0),
    (0, -1, 1.0),
    (1, 0, 1.0),
    (-1, 0, 1.0),
    (1, 1, 0.5),
    (1, -1, 0.5),
    (-1, 1, 0.5),
    (-1, -1, 0.5),
)


def padded_2(block, sides, width):
    for axis, dim in sides:
        count = lax.axis_size(axis)
        forward = [(i, i + 1) for i in range(count - 1)]
        forward.append((count - 1, 0))
        backward = [(target, source) for source, target in forward]
        low = lax.ppermute(
            lax.slice_in_dim(block, block.shape[dim] - width, None, axis=dim), axis, forward
        )
        high = lax.ppermute(lax.slice_in_dim(block, 0, width, axis=dim), axis, backward)
        block = jnp.concatenate([low, block, high], axis=dim)
    return block


def offset(array, row_step, col_step):
    rows = array.shape[-2] - 2
    cols = array.shape[-1] - 2
    return array[..., 1 + row_step : 1 + row_step + rows, 1 + col_step : 1 + col_step + cols]


def interior(array):
    return offset(array, 0, 0)


def laplace(field, mask):
    center = interior(field)
    mask_mid = interior(mask)
    result = jnp.zeros_like(center)
    for row_step, col_step in SIDES:
        result = result + mask_mid * offset(mask, row_step, col_step) * (
            offset(field, row_step, col_step) - center
        )
    return result


def biharmonic(field, mask):
    first = interior(mask) * laplace(field, mask)
    return laplace(first, interior(mask))


def advect(tracer, eastward, northward, mask):
    center = interior(tracer)
    mask_mid = interior(mask)
    result = jnp.zeros_like(center)
    for row_step, col_step in SIDES:
        speed = northward if row_step != 0 else eastward
        orient = float(row_step + col_step)
        face = (
            mask_mid
            * offset(mask, row_step, col_step)
            * 0.5
            * (interior(speed) + offset(speed, row_step, col_step))
        )
        result = result + orient * face * 0.5 * (center + offset(tracer, row_step, col_step))
    return result


def gradient(pressure, mask, row_step, col_step):
    center = interior(pressure)
    mask_mid = interior(mask)
    ahead = (
        mask_mid
        * offset(mask, row_step, col_step)
        * (offset(pressure, row_step, col_step) - center)
    )
    behind = (
        mask_mid
        * offset(mask, -row_step, -col_step)
        * (center - offset(pressure, -row_step, -col_step))
    )
    return 0.5 * (ahead + behind)


def pressure_field(fields):
    density = (-HEAT_EXPANSION * fields[0] + SALT_CONTRACTION * fields[1]) * fields[8]
    return PRESSURE_SCALE * jnp.cumsum(density, axis=0)


def coriolis_rows(first_row, count, rows_global):
    rows = (first_row + jnp.arange(count, dtype=jnp.int32)).astype(jnp.float32)
    return (2.0 * (rows + 0.5) / rows_global - 1.0)[:, None]


def evolve(fields, pressure, coriolis):
    mask_two = fields[8]
    mask_one = interior(mask_two)
    mask_zero = interior(mask_one)
    temp_now = interior(fields[0])
    salt_now = interior(fields[1])
    east_now = interior(fields[2])
    north_now = interior(fields[3])
    press_one = interior(pressure)
    cor_zero = coriolis[2:-2]
    temp_next = mask_zero * (
        interior(interior(fields[4]))
        + STEP_TWICE
        * (
            -advect(temp_now, east_now, north_now, mask_one)
            - TRACER_MIX * biharmonic(fields[4], mask_two)
        )
    )
    salt_next = mask_zero * (
        interior(interior(fields[5]))
        + STEP_TWICE
        * (
            -advect(salt_now, east_now, north_now, mask_one)
            - TRACER_MIX * biharmonic(fields[5], mask_two)
        )
    )
    east_next = mask_zero * (
        interior(interior(fields[6]))
        + STEP_TWICE
        * (
            cor_zero * interior(north_now)
            - gradient(press_one, mask_one, 0, 1)
            - MOMENTUM_MIX * biharmonic(fields[6], mask_two)
        )
    )
    north_next = mask_zero * (
        interior(interior(fields[7]))
        + STEP_TWICE
        * (
            -cor_zero * interior(east_now)
            - gradient(press_one, mask_one, 1, 0)
            - MOMENTUM_MIX * biharmonic(fields[7], mask_two)
        )
    )
    return jnp.stack([temp_next, salt_next, east_next, north_next], 0)


def divergence_source(transports, top_band):
    east_part = 0.5 * (offset(transports[0], 0, 1) - offset(transports[0], 0, -1))
    north_part = 0.5 * (offset(transports[1], 1, 0) - offset(transports[1], -1, 0))
    return -interior(top_band) * (east_part + north_part)


def couplings(depth_band, top_band):
    weights = []
    diagonal = jnp.full(interior(depth_band).shape, SURFACE_TERM, jnp.float32)
    for row_step, col_step, factor in ALL_SIDES:
        weight = (
            factor
            * 0.5
            * (interior(depth_band) + offset(depth_band, row_step, col_step))
            * interior(top_band)
            * offset(top_band, row_step, col_step)
        )
        weights.append(weight)
        diagonal = diagonal + weight
    return (weights, diagonal)


def apply_operator(padded, weights, diagonal):
    result = diagonal * interior(padded)
    for number, (row_step, col_step, factor) in enumerate(ALL_SIDES):
        result = result - weights[number] * offset(padded, row_step, col_step)
    return result


def clip_poles(array, margin, lat_rows):
    global_rows = (
        lax.axis_index("gy") * lat_rows - margin + jnp.arange(array.shape[-2], dtype=jnp.int32)
    )
    keep = (global_rows >= 0) & (global_rows < lat_rows * lax.axis_size("gy"))
    return array * keep.astype(array.dtype)[:, None]


def rim(block, width, rows, cols, lat_rows):
    block = padded_2(block, (("gx", cols), ("gy", rows)), width)
    return clip_poles(block, width, lat_rows)


def neighbour_sum(padded, weights):
    result = jnp.zeros_like(interior(padded))
    for number, (row_step, col_step, factor) in enumerate(ALL_SIDES):
        keep = weights[number]
        result = result + keep * offset(padded, row_step, col_step)
    return result


def trim(array, width):
    if width == 0:
        return array
    return array[..., width:-width, width:-width]


CENTER = 0.2
HALF = 0.6


def basis(start, weights, diagonal):
    inverse = 1.0 / diagonal
    found = [start]
    for step in range(ITERS):
        last = found[-1]
        kept = [trim(weight, step) for weight in weights]
        image = neighbour_sum(last, kept) * trim(inverse, step)
        image = (image - CENTER * interior(last)) * (1.0 / HALF)
        if step > 0:
            image = 2.0 * image - trim(found[-2], 2)
        found.append(image)
    return [trim(term, ITERS - number) for number, term in enumerate(found)]


def total(values):
    count = values.shape[0]
    for axis in ("gy", "gx"):
        size = lax.axis_size(axis)
        spread = jnp.broadcast_to(values[None], (size, count))
        values = jnp.sum(lax.all_to_all(spread, axis, 0, 0, tiled=True), 0)
    return values


def shifted_times(coefs):
    out = [0.0] * (ITERS + 1)
    for j in range(ITERS):
        out[j] = out[j] + CENTER * coefs[j]
        if j == 0:
            out[1] = out[1] + HALF * coefs[0]
        else:
            out[j + 1] = out[j + 1] + 0.5 * HALF * coefs[j]
            out[j - 1] = out[j - 1] + 0.5 * HALF * coefs[j]
    return out


def dot(left, gram, right):
    result = 0.0
    for i, a in enumerate(left):
        for j, b in enumerate(right):
            if isinstance(a, float) and a == 0.0 or isinstance(b, float) and b == 0.0:
                continue
            result = result + a * b * gram[min(i, j), max(i, j)]
    return result


def conjugate_gradients(gram):
    size = ITERS + 1
    z = [1.0] + [0.0] * ITERS
    p = [0.0] * size
    q = [0.0] * size
    x = [0.0] * size
    descent_old = step_old = None
    for iteration in range(ITERS):
        moved = shifted_times(z)
        w = [a - b for a, b in zip(z, moved)]
        descent = dot(z, gram, z)
        curvature = dot(w, gram, z)
        if iteration == 0:
            step_length = descent / curvature
            p, q = list(z), list(w)
        else:
            blend = descent / descent_old
            step_length = descent / (curvature - blend * descent / step_old)
            p = [a + blend * b for a, b in zip(z, p)]
            q = [a + blend * b for a, b in zip(w, q)]
        x = [a + step_length * b for a, b in zip(x, p)]
        z = [a - step_length * b for a, b in zip(z, q)]
        descent_old, step_old = descent, step_length
    return x, z


def on_device(tracer_now, velocity_now, tracer_old, velocity_old, depth_levels, land_blocks):
    levels = tracer_now.shape[1]
    lat_rows = tracer_now.shape[2]
    open_cells = jnp.repeat(jnp.repeat(land_blocks, BLOCK, 0), BLOCK, 1)
    wide = ITERS + 1
    margin = 2
    depths = rim((depth_levels * open_cells).astype(jnp.float32), wide, 0, 1, lat_rows)
    level_index = jnp.arange(levels, dtype=jnp.int32)[:, None, None].astype(jnp.float32)
    wet = (level_index < trim(depths, wide - margin)[None]).astype(jnp.float32)
    fields = jnp.concatenate([tracer_now, velocity_now, tracer_old, velocity_old], 0)
    padded = rim(fields, margin, 2, 3, lat_rows)
    padded = jnp.concatenate([padded, wet[None]], 0)
    first_row = lax.axis_index("gy") * lat_rows - margin
    coriolis = coriolis_rows(first_row, padded.shape[-2], lat_rows * lax.axis_size("gy"))
    pressure = pressure_field(padded)
    updated = evolve(padded, pressure, coriolis)
    depth_band = depths / levels
    top_band = (depths > 0).astype(jnp.float32)
    summed = jnp.sum(updated[2:4], 1) / levels
    transports = rim(summed, wide, 1, 2, lat_rows)
    source = divergence_source(transports, top_band)
    weights, diagonal = couplings(depth_band, top_band)
    terms = basis(source / diagonal, [trim(weight, 1) for weight in weights], trim(diagonal, 1))
    diagonal = trim(diagonal, ITERS)
    sums = []
    for i in range(ITERS + 1):
        scaled = diagonal * terms[i]
        for j in range(i, ITERS + 1):
            sums.append(jnp.sum(scaled * terms[j]))
    sums = total(jnp.stack(sums))
    gram = {}
    count = 0
    for i in range(ITERS + 1):
        for j in range(i, ITERS + 1):
            gram[i, j] = sums[count]
            count += 1
    x, z = conjugate_gradients(gram)
    height = sum(c * term for c, term in zip(x[:ITERS], terms))
    residual = diagonal * sum(c * term for c, term in zip(z, terms))
    return (updated[0:2], updated[2:4], height, residual)


def solution(mesh):
    in_specs = (
        P(None, None, "gy", "gx"),
        P(None, None, "gy", "gx"),
        P(None, None, "gy", "gx"),
        P(None, None, "gy", "gx"),
        P("gy", "gx"),
        P("gy", "gx"),
    )
    out_specs = (P(None, None, "gy", "gx"), P(None, None, "gy", "gx"), P("gy", "gx"), P("gy", "gx"))
    return jax.shard_map(
        on_device, mesh=mesh, in_specs=in_specs, out_specs=out_specs, check_vma=False
    )
```

```python
import jax
import jax.numpy as jnp
from jax import lax
from jax.experimental import pallas as pl
from jax.experimental.pallas import tpu as pltpu
from jax.sharding import PartitionSpec as P

ITERS = 4
STEP_TWICE = 0.1
TRACER_MIX = 0.05
MOMENTUM_MIX = 0.05
HEAT_EXPANSION = 0.2
SALT_CONTRACTION = 0.15
PRESSURE_SCALE = 0.2
SURFACE_TERM = 1.0
ALL_SIDES = (
    (0, 1, 1.0),
    (0, -1, 1.0),
    (1, 0, 1.0),
    (-1, 0, 1.0),
    (1, 1, 0.5),
    (1, -1, 0.5),
    (-1, 1, 0.5),
    (-1, -1, 0.5),
)
CENTER = 0.2
HALF = 0.6

LEVELS = 32
ROWS = 16
LANES = 128
BAND = 8
F32 = jnp.float32

NEAR, FAR, NOW = 0, 4, 8
ROW_DEPTH = 12 * LEVELS
ROW_SIZE = ROW_DEPTH + BAND
COL_CORNER = 4 * ROWS
COL_TALL = COL_CORNER + 8
COL_DEPTH = COL_TALL + LEVELS
COL_SIZE = COL_DEPTH + 2 * BAND + ROWS


def iota(shape, dim):
    return lax.broadcasted_iota(jnp.int32, shape, dim)


def roll(x, shift, axis):
    return pltpu.roll(x, shift % x.shape[axis] if isinstance(shift, int) else shift, axis)


def call(kernel, outs, scratch=(), flops=0, count=1):
    vmem = pl.BlockSpec(memory_space=pltpu.VMEM)
    return pl.pallas_call(
        kernel,
        out_shape=tuple(jax.ShapeDtypeStruct(o, F32) for o in outs),
        in_specs=[vmem] * count,
        out_specs=tuple(vmem for _ in outs),
        scratch_shapes=list(scratch),
        compiler_params=pltpu.CompilerParams(vmem_limit_bytes=32 * 1024 * 1024),
        cost_estimate=pl.CostEstimate(flops=flops, bytes_accessed=1 << 20, transcendentals=0),
    )


def rows_kernel(tn, vn, to, vo, depth, land, first, last, deff):
    for name, near, far in ((first, 0, 1), (last, ROWS - 1, ROWS - 2)):
        for f in range(4):
            old = (to, vo)[f // 2]
            now = (tn, vn)[f // 2]
            for slot, ref, row in ((NEAR, old, near), (FAR, old, far), (NOW, now, near)):
                name[pl.ds((slot + f) * LEVELS, LEVELS), :] = ref[f % 2, :, row, :]
    blocks = land[...].astype(F32)
    spread = (iota((blocks.shape[1], LANES), 1) // 8 == iota((blocks.shape[1], LANES), 0)).astype(F32)
    opened = jnp.dot(blocks, spread, preferred_element_type=F32)
    lower = jnp.broadcast_to(opened[0:1], (BAND, LANES))
    upper = jnp.broadcast_to(opened[1:2], (BAND, LANES))
    deff[0:BAND, :] = depth[0:BAND, :].astype(F32) * lower
    deff[BAND:ROWS, :] = depth[BAND:ROWS, :].astype(F32) * upper
    first[ROW_DEPTH:ROW_SIZE, :] = deff[0:BAND, :]
    last[ROW_DEPTH:ROW_SIZE, :] = deff[BAND:ROWS, :]


def columns_kernel(tn, vn, to, vo, east, west):
    pair = iota((ROWS, LANES), 1) // 2

    def level(k, held):
        held = list(held)
        for q, ref in enumerate((to, vo, tn, vn)):
            for f in range(2):
                spot = k + LEVELS * f
                moved = roll(ref[f, k], 2 * spot, 1)
                held[q] = jnp.where(pair == lax.rem(spot + 63, 64), moved, held[q])
                held[4 + q] = jnp.where(pair == spot, moved, held[4 + q])
        return tuple(held)

    zero = jnp.zeros((ROWS, LANES), F32)
    held = lax.fori_loop(0, LEVELS, level, (zero,) * 8, unroll=4)
    for q in range(4):
        east[pl.ds(q * ROWS, ROWS), :] = held[q]
        west[pl.ds(q * ROWS, ROWS), :] = held[4 + q]


def corners_kernel(ceast, cwest, low, high, deff, east, west):
    level = iota((LEVELS, LANES), 0)
    lane = iota((LEVELS, LANES), 1)
    for out, main, column, shift in ((east, ceast, LANES - 1, -1), (west, cwest, 0, 0)):
        out[0:COL_CORNER, :] = main[...]
        tall = jnp.zeros((LEVELS, LANES), F32)
        flat = []
        for q in range(2):
            for side, rim in enumerate((low, high)):
                row = jnp.zeros((LEVELS, LANES), F32)
                for f in range(2):
                    near = rim[pl.ds((NEAR + 2 * q + f) * LEVELS, LEVELS), :]
                    wide = jnp.broadcast_to(near[:, column : column + 1], (LEVELS, LANES))
                    spot = (2 * (level + LEVELS * f) + shift + LANES) % LANES
                    row = jnp.where(lane == spot, wide, row)
                    tall = jnp.where(lane == 4 * q + 2 * f + side, wide, tall)
                flat.append(jnp.sum(row, axis=0, keepdims=True))
        flat.append(jnp.zeros((4, LANES), F32))
        out[COL_CORNER:COL_TALL, :] = jnp.concatenate(flat, axis=0)
        out[COL_TALL:COL_DEPTH, :] = tall
        out[COL_DEPTH : COL_DEPTH + BAND, :] = low[ROW_DEPTH:ROW_SIZE, :]
        out[COL_DEPTH + BAND : COL_DEPTH + BAND + ROWS, :] = deff[...]
        out[COL_DEPTH + BAND + ROWS : COL_SIZE, :] = high[ROW_DEPTH:ROW_SIZE, :]


class Rims:
    def __init__(self, low, high, own_east, own_west, from_west, from_east):
        self.low, self.high = low, high
        self.refs = (own_east, own_west, from_west, from_east)
        lane = iota((ROWS, LANES), 1)
        self.even = lane % 2 == 0
        self.packed = ((lane % 64) // 2).astype(F32)
        self.lane, self.row = lane, iota((ROWS, LANES), 0)
        tall = (2 * BAND + ROWS, LANES)
        lane = iota(tall, 1)
        own = own_east[COL_DEPTH:COL_SIZE, :]
        east = from_east[COL_DEPTH:COL_SIZE, :]
        west = from_west[COL_DEPTH:COL_SIZE, :]

        def column(tile, at):
            return jnp.broadcast_to(tile[:, at : at + 1], tall)

        beyond_e = column(east, 0)
        beyond_w = column(west, LANES - 1)
        self.depth = own
        self.min_e = jnp.minimum(own, jnp.where(lane == LANES - 1, beyond_e, roll(own, -1, 1)))
        self.min_w = jnp.minimum(own, jnp.where(lane == 0, beyond_w, roll(own, 1, 1)))
        self.min_n = jnp.minimum(own, roll(own, -1, 0))
        self.min_s = jnp.minimum(own, roll(own, 1, 0))
        even = lane % 2 == 0
        center = jnp.where(even, beyond_e, beyond_w)
        outer = jnp.where(even, column(east, 1), column(west, LANES - 2))
        inner = jnp.where(even, column(own, LANES - 1), column(own, 0))
        mid = slice(BAND, BAND + ROWS)
        self.side_depth = center[mid]
        self.side_faces = [
            (self.packed < jnp.minimum(center, other)[mid]).astype(F32)
            for other in (outer, inner, roll(center, -1, 0), roll(center, 1, 0))
        ]
        self.mids = [a[mid] for a in (own, self.min_e, self.min_w, self.min_n, self.min_s)]

    def shifted_rows(self, x, below, above):
        return (
            jnp.where(self.row == ROWS - 1, above, roll(x, -1, 0)),
            jnp.where(self.row == 0, below, roll(x, 1, 0)),
        )

    def shifted_columns(self, x, beyond):
        return (
            jnp.where(self.lane == LANES - 1, beyond, roll(x, -1, 1)),
            jnp.where(self.lane == 0, beyond, roll(x, 1, 1)),
        )

    def beside(self, q):
        _, _, from_west, from_east = self.refs
        at = pl.ds(q * ROWS, ROWS)
        return jnp.where(self.even, from_east[at, :], roll(from_west[at, :], 2, 1))

    def first_columns(self, q):
        own_east, own_west, from_west, from_east = self.refs
        at = pl.ds(q * ROWS, ROWS)
        near = self.beside(q)
        far = jnp.where(self.even, roll(from_east[at, :], -1, 1), roll(from_west[at, :], 3, 1))
        own = roll(jnp.where(self.even, own_west[at, :], own_east[at, :]), 1, 1)

        def corner(side):
            spot = slice(COL_CORNER + 2 * q + side, COL_CORNER + 2 * q + side + 1)
            row = jnp.where(self.even[0:1], from_east[spot, :], roll(from_west[spot, :], 2, 1))
            return jnp.broadcast_to(row, (ROWS, LANES))

        above, below = self.shifted_rows(near, corner(0), corner(1))
        result = 0.0
        for face, other in zip(self.side_faces, (far, own, above, below)):
            result = result + face * (other - near)
        return result

    def first_row(self, q, f, side, inner):
        _, _, from_west, from_east = self.refs
        rim = (self.low, self.high)[side]
        row = (BAND - 1, BAND + ROWS)[side]
        near = rim[pl.ds((NEAR + 2 * q + f) * LEVELS, LEVELS), :]
        far = rim[pl.ds((FAR + 2 * q + f) * LEVELS, LEVELS), :]
        shape = (LEVELS, LANES)
        level = iota(shape, 0).astype(F32)
        lane = iota(shape, 1)
        spot = 4 * q + 2 * f + side
        tall = slice(COL_TALL, COL_DEPTH)
        corner_e = jnp.broadcast_to(from_east[tall, :][:, spot : spot + 1], shape)
        corner_w = jnp.broadcast_to(from_west[tall, :][:, spot : spot + 1], shape)
        east = jnp.where(lane == LANES - 1, corner_e, roll(near, -1, 1))
        west = jnp.where(lane == 0, corner_w, roll(near, 1, 1))
        above, below = (inner, far) if side == 0 else (far, inner)
        result = 0.0
        for bound, other in (
            (self.min_e, east),
            (self.min_w, west),
            (self.min_n, above),
            (self.min_s, below),
        ):
            face = (level < bound[row : row + 1]).astype(F32)
            result = result + face * (other - near)
        return result


def laplace(rims, x, faces, beyond, below, above):
    east, west = rims.shifted_columns(x, beyond)
    north, south = rims.shifted_rows(x, below, above)
    e, w, n, s = faces
    return e * (east - x) + w * (west - x) + (n * (north - x) + s * (south - x))


def prepare(rims, q, old, sides, rowsides):
    sides[pl.ds(0, ROWS), :] = rims.beside(q)
    sides[pl.ds(ROWS, ROWS), :] = rims.first_columns(q)
    for f in range(2):
        for side, row in ((0, 0), (1, ROWS - 1)):
            spot = pl.ds((2 * f + side) * LEVELS, LEVELS)
            rowsides[spot, :] = rims.first_row(q, f, side, old[f, :, row, :])


def level_faces(rims, k):
    level = k.astype(F32)
    return [(level < bound).astype(F32) for bound in rims.mids]


def biharmonic(rims, q, f, k, x, faces, sides, rowsides):
    shift = lax.rem(2 * LANES - 1 - 2 * k - 64 * f, LANES)
    beyond = roll(sides[pl.ds(0, ROWS), :], shift, 1)
    first_beyond = roll(sides[pl.ds(ROWS, ROWS), :], shift, 1)
    spot = (NEAR + 2 * q + f) * LEVELS + k
    first = laplace(
        rims, x, faces, beyond, rims.low[pl.ds(spot, 1), :], rims.high[pl.ds(spot, 1), :]
    )
    at = 2 * f * LEVELS + k
    return laplace(
        rims,
        first,
        faces,
        first_beyond,
        rowsides[pl.ds(at, 1), :],
        rowsides[pl.ds(at + LEVELS, 1), :],
    )


def velocity_kernel(
    tn, vn, vo, low, high, own_east, own_west, from_west, from_east, cor_ref,
    out, first, last, own, sides, rowsides, dens,
):
    rims = Rims(low, high, own_east, own_west, from_west, from_east)
    prepare(rims, 1, vo, sides, rowsides)
    packed = rims.beside(2)
    packed = HEAT_EXPANSION * -packed + SALT_CONTRACTION * roll(packed, 64, 1)
    packed = PRESSURE_SCALE * packed * (rims.packed < rims.side_depth).astype(F32)
    sides[pl.ds(2 * ROWS, ROWS), :] = packed
    level = iota((LEVELS, LANES), 0).astype(F32)
    for side, rim, row in ((0, low, BAND - 1), (1, high, BAND + ROWS)):
        temp = rim[pl.ds(NOW * LEVELS, LEVELS), :]
        salt = rim[pl.ds((NOW + 1) * LEVELS, LEVELS), :]
        wet = (level < rims.depth[row : row + 1]).astype(F32)
        term = (SALT_CONTRACTION * salt - HEAT_EXPANSION * temp) * wet
        dens[pl.ds(side * LEVELS, LEVELS), :] = PRESSURE_SCALE * term
    cor = cor_ref[...]

    def step(k, carry):
        press, press_side, press_low, press_high, sum_e, sum_n = carry
        faces = level_faces(rims, k)
        wet, faces = faces[0], faces[1:]
        e, w, n, s = faces
        term = (SALT_CONTRACTION * tn[1, k] - HEAT_EXPANSION * tn[0, k]) * wet
        press = press + PRESSURE_SCALE * term
        shift = LANES - 1 - 2 * k
        press_side = press_side + roll(sides[pl.ds(2 * ROWS, ROWS), :], shift, 1)
        press_low = press_low + dens[pl.ds(k, 1), :]
        press_high = press_high + dens[pl.ds(LEVELS + k, 1), :]
        east, west = rims.shifted_columns(press, press_side)
        north, south = rims.shifted_rows(press, press_low, press_high)
        slope_x = 0.5 * (e * (east - press) + w * (press - west))
        slope_y = 0.5 * (n * (north - press) + s * (press - south))
        turns = (cor * vn[1, k] - slope_x, -cor * vn[0, k] - slope_y)
        nexts = []
        for f in range(2):
            x = vo[f, k]
            mixed = biharmonic(rims, 1, f, k, x, faces, sides, rowsides)
            value = wet * (x + STEP_TWICE * (turns[f] - MOMENTUM_MIX * mixed))
            out[f, k] = value
            nexts.append(value)
        return press, press_side, press_low, press_high, sum_e + nexts[0], sum_n + nexts[1]

    zero = jnp.zeros((ROWS, LANES), F32)
    line = jnp.zeros((1, LANES), F32)
    carry = lax.fori_loop(0, LEVELS, step, (zero, zero, line, line, zero, zero), unroll=2)
    for f in range(2):
        total = carry[4 + f] * (1.0 / LEVELS)
        own[pl.ds(f * ROWS, ROWS), :] = total
        first[pl.ds(f * BAND, BAND), :] = total[0:BAND]
        last[pl.ds(f * BAND, BAND), :] = total[BAND:ROWS]


def tracer_kernel(
    tn, vn, to, low, high, own_east, own_west, from_west, from_east, out, sides, rowsides,
):
    rims = Rims(low, high, own_east, own_west, from_west, from_east)
    prepare(rims, 0, to, sides, rowsides)
    sides[pl.ds(2 * ROWS, ROWS), :] = rims.beside(2)
    sides[pl.ds(3 * ROWS, ROWS), :] = rims.beside(3)

    def step(k, carry):
        faces = level_faces(rims, k)
        wet, faces = faces[0], faces[1:]
        e, w, n, s = faces
        eastward, northward = vn[0, k], vn[1, k]
        shift = LANES - 1 - 2 * k
        beyond = roll(sides[pl.ds(3 * ROWS, ROWS), :], shift, 1)
        east, west = rims.shifted_columns(eastward, beyond)
        spot = (NOW + 3) * LEVELS + k
        north, south = rims.shifted_rows(
            northward, low[pl.ds(spot, 1), :], high[pl.ds(spot, 1), :]
        )
        flow_e = 0.25 * e * (eastward + east)
        flow_w = 0.25 * w * (eastward + west)
        flow_n = 0.25 * n * (northward + north)
        flow_s = 0.25 * s * (northward + south)
        for f in range(2):
            c = tn[f, k]
            beyond = roll(sides[pl.ds(2 * ROWS, ROWS), :], lax.rem(shift + LANES - 64 * f, LANES), 1)
            east, west = rims.shifted_columns(c, beyond)
            spot = (NOW + f) * LEVELS + k
            north, south = rims.shifted_rows(c, low[pl.ds(spot, 1), :], high[pl.ds(spot, 1), :])
            moved = flow_e * (c + east) - flow_w * (c + west)
            moved = moved + flow_n * (c + north) - flow_s * (c + south)
            x = to[f, k]
            mixed = biharmonic(rims, 0, f, k, x, faces, sides, rowsides)
            out[f, k] = wet * (x + STEP_TWICE * (-moved - TRACER_MIX * mixed))
        return carry

    lax.fori_loop(0, LEVELS, step, 0, unroll=2)


TALL = 2 * BAND + ROWS
GRAM = [(i, j) for i in range(ITERS + 1) for j in range(i, ITERS + 1)]


def moved(x, row_step, col_step):
    if row_step:
        x = roll(x, -row_step, 0)
    if col_step:
        x = roll(x, -col_step, 1)
    return x


def basis_kernel(own, from_west, from_east, own_cols, west_cols, east_cols, terms, sums):
    lane = iota((TALL, LANES), 1)

    def ring(mine, west, east):
        return jnp.concatenate([mine, jnp.where(lane < LANES // 2, east, west)], axis=1)

    eastward = ring(*(ref[0:TALL, :] for ref in (own, from_west, from_east)))
    northward = ring(*(ref[TALL : 2 * TALL, :] for ref in (own, from_west, from_east)))
    deep = slice(COL_DEPTH, COL_SIZE)
    levels = ring(*(ref[deep, :] for ref in (own_cols, west_cols, east_cols)))
    depth = levels * (1.0 / LEVELS)
    top = (levels > 0).astype(F32)
    source = -top * (
        0.5 * (moved(eastward, 0, 1) - moved(eastward, 0, -1))
        + 0.5 * (moved(northward, 1, 0) - moved(northward, -1, 0))
    )
    depth_cols = {step: moved(depth, 0, step) for step in (-1, 0, 1)}
    top_cols = {step: moved(top, 0, step) for step in (-1, 0, 1)}
    weights = []
    diagonal = jnp.full(depth.shape, SURFACE_TERM, F32)
    for row_step, col_step, factor in ALL_SIDES:
        weight = (
            (factor * 0.5)
            * (depth + moved(depth_cols[col_step], row_step, 0))
            * top
            * moved(top_cols[col_step], row_step, 0)
        )
        weights.append(weight)
        diagonal = diagonal + weight
    inverse = 1.0 / diagonal
    weights = [weight * (inverse * (1.0 / HALF)) for weight in weights]
    found = [source / diagonal]
    for step in range(ITERS):
        last = found[-1]
        cols = {s: moved(last, 0, s) for s in (-1, 0, 1)}
        image = last * (-CENTER / HALF)
        for weight, (row_step, col_step, _) in zip(weights, ALL_SIDES):
            image = image + weight * moved(cols[col_step], row_step, 0)
        found.append(image if step == 0 else 2.0 * image - found[-2])
    mine = [term[BAND : BAND + ROWS, 0:LANES] for term in found]
    diagonal = diagonal[BAND : BAND + ROWS, 0:LANES]
    for number, term in enumerate(mine + [diagonal]):
        terms[pl.ds(number * ROWS, ROWS), :] = term
    scaled = [diagonal * term for term in mine]
    products = []
    for i, j in GRAM:
        product = scaled[i] * mine[j]
        products.append(jnp.sum(product, axis=0, keepdims=True))
    products.append(jnp.zeros((16 - len(GRAM), LANES), F32))
    stacked = jnp.sum(jnp.concatenate(products, axis=0), axis=1, keepdims=True)
    spot = iota((16, LANES), 1) == iota((16, LANES), 0)
    line = jnp.sum(jnp.where(spot, jnp.broadcast_to(stacked, (16, LANES)), 0.0), axis=0, keepdims=True)
    sums[...] = jnp.broadcast_to(line, sums.shape)


def relay_kernel(found, out):
    line = jnp.sum(found[...], axis=0, keepdims=True)
    out[...] = jnp.broadcast_to(line, out.shape)


def basis_image(coefs):
    out = [0.0] * (ITERS + 1)
    for j in range(ITERS):
        out[j] = out[j] + CENTER * coefs[j]
        if j == 0:
            out[1] = out[1] + HALF * coefs[0]
        else:
            out[j + 1] = out[j + 1] + 0.5 * HALF * coefs[j]
            out[j - 1] = out[j - 1] + 0.5 * HALF * coefs[j]
    return out


def is_zero(value):
    return isinstance(value, float) and value == 0.0


def inner(left, gram, right):
    result = 0.0
    for i, a in enumerate(left):
        if is_zero(a):
            continue
        part = 0.0
        for j, b in enumerate(right):
            if not is_zero(b):
                part = part + b * gram[min(i, j), max(i, j)]
        result = result + a * part
    return result


def conjugate_gradients(gram):
    size = ITERS + 1
    z = [1.0] + [0.0] * ITERS
    p = [0.0] * size
    q = [0.0] * size
    x = [0.0] * size
    descent_old = step_old = None
    for iteration in range(ITERS):
        image = [a - b for a, b in zip(z, basis_image(z))]
        descent = inner(z, gram, z)
        curvature = inner(image, gram, z)
        if iteration == 0:
            length = descent / curvature
            p, q = list(z), list(image)
        else:
            blend = descent / descent_old
            length = descent / (curvature - blend * descent / step_old)
            p = [a + blend * b for a, b in zip(z, p)]
            q = [a + blend * b for a, b in zip(image, q)]
        x = [a + length * b for a, b in zip(x, p)]
        z = [a - length * b for a, b in zip(z, q)]
        descent_old, step_old = descent, length
    return x, z


def finish_kernel(found, terms, height, residual):
    line = jnp.sum(found[...], axis=0, keepdims=True)
    gram = {}
    for number, key in enumerate(GRAM):
        gram[key] = jnp.broadcast_to(line[:, number : number + 1], (1, LANES))
    x, z = conjugate_gradients(gram)
    tall = 0.0
    rest = 0.0
    for number in range(ITERS + 1):
        term = terms[pl.ds(number * ROWS, ROWS), :]
        if number < ITERS:
            tall = tall + x[number] * term
        rest = rest + z[number] * term
    height[...] = tall
    residual[...] = rest * terms[pl.ds((ITERS + 1) * ROWS, ROWS), :]


def exchange(to_less, to_more, axis, cyclic):
    count = lax.axis_size(axis)
    up = [(i, i + 1) for i in range(count - 1)]
    if cyclic:
        up.append((count - 1, 0))
    down = [(b, a) for a, b in up]
    return lax.ppermute(to_more, axis, up), lax.ppermute(to_less, axis, down)


def on_device(tracer_now, velocity_now, tracer_old, velocity_old, depth_levels, land_blocks):
    fields = (tracer_now, velocity_now, tracer_old, velocity_old)
    tile = (ROWS, LANES)
    first, last, deff = call(rows_kernel, ((ROW_SIZE, LANES), (ROW_SIZE, LANES), tile), count=6)(
        *fields, depth_levels, land_blocks
    )
    low, high = exchange(first, last, "gy", False)
    east, west = call(columns_kernel, ((4 * ROWS, LANES),) * 2, flops=10**7, count=4)(*fields)
    own_east, own_west = call(corners_kernel, ((COL_SIZE, LANES),) * 2, count=5)(
        east, west, low, high, deff
    )
    from_west, from_east = exchange(own_west, own_east, "gx", True)
    row = (lax.axis_index("gy") * ROWS + iota(tile, 0)).astype(F32)
    cor = 2.0 * (row + 0.5) / (ROWS * lax.axis_size("gy")) - 1.0
    rims = (low, high, own_east, own_west, from_west, from_east)
    velocity, first, last, own = call(
        velocity_kernel,
        (velocity_old.shape, tile, tile, (2 * ROWS, LANES)),
        (
            pltpu.VMEM((3 * ROWS, LANES), F32),
            pltpu.VMEM((4 * LEVELS, LANES), F32),
            pltpu.VMEM((2 * LEVELS, LANES), F32),
        ),
        flops=2 * 10**7,
        count=10,
    )(tracer_now, velocity_now, velocity_old, *rims, cor)
    tracer = call(
        tracer_kernel,
        (tracer_old.shape,),
        (pltpu.VMEM((4 * ROWS, LANES), F32), pltpu.VMEM((4 * LEVELS, LANES), F32)),
        flops=2 * 10**7,
        count=9,
    )(tracer_now, velocity_now, tracer_old, *rims)[0]
    below, above = exchange(first, last, "gy", False)
    wide = jnp.concatenate(
        [below[:BAND], own[:ROWS], above[:BAND], below[BAND:], own[ROWS:], above[BAND:]], 0
    )
    wide_west, wide_east = exchange(wide, wide, "gx", True)
    terms, sums = call(
        basis_kernel,
        (((ITERS + 2) * ROWS, LANES), (lax.axis_size("gx"), LANES)),
        count=6,
    )(wide, wide_west, wide_east, own_east, from_west, from_east)
    sums = lax.all_to_all(sums, "gx", 0, 0, tiled=True)
    sums = call(relay_kernel, ((lax.axis_size("gy"), LANES),), count=1)(sums)[0]
    sums = lax.all_to_all(sums, "gy", 0, 0, tiled=True)
    height, residual = call(finish_kernel, (tile, tile), count=2)(sums, terms)
    return (tracer, velocity, height, residual)


def solution(mesh):
    field = P(None, None, "gy", "gx")
    flat = P("gy", "gx")
    return jax.shard_map(
        on_device,
        mesh=mesh,
        in_specs=(field, field, field, field, flat, flat),
        out_specs=(field, field, flat, flat),
        check_vma=False,
    )
```
